256 devices in a mesh: cohort: 64 (over x, z, y_hi), variant: 4 (over y_lo, core).
Axes of the slice: x: 4, y: 4 (y_hi: 2, y_lo: 2; y = y_hi * 2 + y_lo), z: 8, core: 2. Of those that a mesh axis runs over, the one named last changes fastest.
Arguments:
- probs: bfloat16 [3, 32768, 3072], P(None, 'cohort', 'variant'), may hold values from 0 to 1, as said below
- cohort_sizes: int32 [42], replicated, may hold values from 1 to 1024, 32768 in all
Outputs:
- kinship: float32 [32768, 2560], P('cohort', 'variant')
The draws below stay inside these ranges and needn't reach their ends.
Inputs may be any that keep to these rules, and one draw needn't show every extreme that they name: `cohort_sizes`: sizes sum to 32768, and the largest cohort has exactly 1024 samples. `probs`: the three probabilities of one call are nonnegative and sum to the call's confidence, at most one up to rounding; a missing call has all three zero.
All inputs are finite; a program needn't handle non-finite values.
Results may differ from the reference program's by a relative error of at most 0.0003.
Values may be sent and summed in bfloat16 or wider, within the bound.
No kernel may reach another device: no remote copies, remote signals or barrier semaphores. Data moves between devices by JAX's collectives and lax.ppermute only.
A program may use at most 128 MiB of HBM per device.

```python
import math
import jax
import jax.numpy as jnp
import numpy as np
from jax import lax

TILE = 512
REACH = 2
VARIANTS = 3072
SAMPLES = 32768
BAND = 2560
MOST = 1024
COHORTS = 42


def draw_probs(key, part):
    key = jax.random.fold_in(key, 11)
    keys = jax.random.split(key, 8)
    het_shift = jax.random.uniform(keys[0], (SAMPLES, 1), minval=-1.5, maxval=1.0)
    freq_shift = jax.random.uniform(keys[6], (1, VARIANTS), minval=-2.0, maxval=2.0)
    logits = jax.random.normal(keys[1], (3, SAMPLES, VARIANTS)) * 1.5
    logits = logits + jnp.stack([-freq_shift + jnp.zeros_like(het_shift), het_shift + jnp.zeros_like(freq_shift), freq_shift + jnp.zeros_like(het_shift)])
    soft = jax.nn.softmax(logits, axis=0)
    confidence = jax.random.uniform(keys[2], (SAMPLES, VARIANTS), minval=0.7, maxval=1.0)
    present = (jax.random.randint(keys[3], (SAMPLES, VARIANTS), 0, 10) > 0).astype(jnp.float32)
    weight = confidence * present
    hom_only = jax.random.randint(keys[4], (SAMPLES, 1), 0, 32) == 0
    calls = jax.random.randint(keys[5], (SAMPLES, VARIANTS), 0, 2).astype(jnp.float32)
    hom_conf = jax.random.uniform(keys[7], (SAMPLES, 1), minval=0.5, maxval=1.0) * (2.0 / jnp.sqrt(jnp.float32(VARIANTS)))
    hard = jnp.stack([(1.0 - calls) * present * hom_conf, jnp.zeros_like(calls), calls * present * hom_conf])
    result = jnp.where(hom_only[None], hard, soft * weight[None])
    return result.astype(jnp.bfloat16)


def length_profile(amount, total, most, slope):
    loads = [(1 << 20) // math.isqrt(standing ** slope) + 1 for standing in range(2, amount + 1)]
    surplus, counts = total - most - (amount - 1), [1] * (amount - 1)
    while surplus > 0:
        candidates = [i for i in range(amount - 1) if counts[i] < most]
        pool, budget = sum([loads[i] for i in candidates]), surplus
        for i in candidates:
            extra = min(most - counts[i], max(1, budget * loads[i] // pool), surplus)
            counts[i] = counts[i] + extra
            surplus = surplus - extra
    return np.array([most] + counts)


def uneven(key, number_of, total, most, slope):
    if number_of == 2:
        one = jax.random.randint(key, (), max(1, total - most), min(most, total - 1) + 1)
        return jnp.stack([one, total - one])
    tallies = jnp.asarray(length_profile(number_of, total, most, slope), jnp.int32)
    couples = (number_of - 1) // 2
    donor, receiver = tallies[1:1 + 2 * couples:2], tallies[2:2 + 2 * couples:2]
    slack = jnp.minimum(donor - 1, most - receiver)
    shifted = jax.random.randint(jax.random.fold_in(key, 1), (couples,), 0, 1 << 20) % (slack + 1)
    tallies = tallies.at[1:1 + 2 * couples:2].set(donor - shifted).at[2:2 + 2 * couples:2].set(receiver + shifted)
    return tallies[jax.random.permutation(jax.random.fold_in(key, 2), number_of)]


def setup_inputs(seed: int = 0) -> dict:
    key_of = jax.random.split(jax.random.key(seed), 3)
    return {
        "probs": draw_probs(jax.random.fold_in(key_of[2], 71), 0),
        "cohort_sizes": uneven(key_of[1], COHORTS, SAMPLES, MOST, 1).astype(jnp.int32),
    }


def cohort_of(positions, cohort_ends):
    return jnp.sum((cohort_ends[None, :] <= positions[:, None]).astype(jnp.int32), axis=1)


def reference(probs, cohort_sizes):
    observed = (probs[0].astype(jnp.float32) + probs[1] + probs[2]).astype(jnp.bfloat16)
    left_num = jnp.concatenate([probs[1], probs[0], probs[2]], axis=1)
    left_den = jnp.concatenate([probs[1], observed], axis=1)
    right_num = jnp.concatenate([probs[1], -2 * probs[2], -2 * probs[0]], axis=1)
    right_den = jnp.concatenate([observed, probs[1]], axis=1)
    margin = REACH * TILE
    right_num = jnp.pad(right_num, ((margin, margin), (0, 0)))
    right_den = jnp.pad(right_den, ((margin, margin), (0, 0)))
    cohort_ends = jnp.cumsum(cohort_sizes).astype(jnp.int32)

    def one_block(block_index):
        start = (block_index * TILE).astype(jnp.int32)
        rows_num = lax.dynamic_slice_in_dim(left_num, start, TILE, 0)
        rows_den = lax.dynamic_slice_in_dim(left_den, start, TILE, 0)
        part_num = lax.dynamic_slice_in_dim(right_num, start, BAND, 0)
        part_den = lax.dynamic_slice_in_dim(right_den, start, BAND, 0)
        numerator = jnp.dot(rows_num, part_num.T, preferred_element_type=jnp.float32)
        denominator = jnp.dot(rows_den, part_den.T, preferred_element_type=jnp.float32)
        row_pos = start + jnp.arange(TILE, dtype=jnp.int32)
        col_pos = start - margin + jnp.arange(BAND, dtype=jnp.int32)
        inside = (col_pos >= 0) & (col_pos < SAMPLES)
        same_cohort = cohort_of(row_pos, cohort_ends)[:, None] == cohort_of(col_pos, cohort_ends)[None, :]
        ratio = numerator / jnp.maximum(denominator, 1.0)
        return jnp.where(same_cohort & inside[None, :], ratio, 0.0)

    blocks = lax.map(one_block, jnp.arange(SAMPLES // TILE, dtype=jnp.int32))
    return blocks.reshape(SAMPLES, BAND)
```

```python
import jax
import jax.numpy as jnp
from jax import lax
from jax.experimental import pallas as pl
from jax.experimental.pallas import tpu as pltpu
from jax.sharding import PartitionSpec as P

AXES = ("cohort", "variant")
TILE = 512
HALF = 256
WIDTH = 640
F32 = jnp.float32


def route(blocks, rule):
    pairs = []
    for k in range(blocks // 2):
        for par in range(2):
            for lo in range(2):
                for core in range(2):
                    to = rule(k, par, lo, core)
                    if to is not None and 0 <= to[0] < blocks // 2:
                        source = (2 * k + par) * 4 + lo * 2 + core
                        pairs.append((source, (2 * to[0] + to[1]) * 4 + to[2] * 2 + to[3]))
    return pairs


def is_a(par, core):
    return core == par


def is_outer(par, lo):
    return lo == par


def to_mate(k, par, lo, core):
    if is_a(par, core):
        return (k, par, lo, 1 - core)
    return (k, 1 - par, lo, core)


def to_next(k, par, lo, core):
    return (k - 1 if core == 0 else k + 1, par, lo, core)


def to_chip(k, par, lo, core):
    return (k, par, 1 - lo, core)


def to_chip_a(k, par, lo, core):
    return (k, par, 1 - lo, core) if is_a(par, core) else None


def to_far(k, par, lo, core):
    return (k + 1 if core == 0 else k - 1, par, lo, 1 - core)


def to_mirror(k, par, lo, core):
    return (k, 1 - par, 1 - lo, 1 - core) if is_a(par, core) else None


def to_cut(k, par, lo, core):
    if is_a(par, core) and is_outer(par, lo):
        return (k + 1 if par == 0 else k - 1, par, lo, core)
    return None


def to_owner(k, par, lo, core):
    if is_a(par, core) == is_outer(par, lo):
        return (k, par, 1 - lo, core)
    return None


def to_core(k, par, lo, core):
    return (k, par, lo, 1 - core)


def dot_t(left, right):
    return lax.dot_general(left, right, (((1,), (1,)), ((), ())), preferred_element_type=F32)


def pair_sums(left, left_obs, right, right_obs):
    cross = dot_t(left[0], right[2]) + dot_t(left[2], right[0])
    num = dot_t(left[1], right[1]) - 2.0 * cross
    den = dot_t(left[1], right_obs[...]) + dot_t(left_obs[...], right[1])
    return num, den


def sums_kernel(role, own, mate, far, send_a, send_b, keep_a, keep_b, tri, own_obs, mate_obs, far_obs):
    par, lo, core = role[0], role[1], role[2]
    kind_a = core == par
    outer = lo == par
    for source, target in ((own, own_obs), (mate, mate_obs), (far, far_obs)):
        total = source[0].astype(F32) + source[1].astype(F32) + source[2].astype(F32)
        target[...] = total.astype(jnp.bfloat16)

    def put(first, second, values):
        for i in range(2):
            first[i] = values[i][:, :HALF]
            second[i] = values[i][:, HALF:]

    @pl.when(kind_a)
    def _():
        near = pair_sums(own, own_obs, mate, mate_obs)

        @pl.when(outer)
        def _():
            put(send_a, send_b, near)

        @pl.when(jnp.logical_not(outer))
        def _():
            put(keep_a, keep_b, near)

        cut = pair_sums(mate, mate_obs, far, far_obs)

        @pl.when(outer)
        def _():
            put(keep_a, keep_b, cut)

        @pl.when(jnp.logical_not(outer))
        def _():
            put(send_a, send_b, cut)

        both = pair_sums(own, own_obs, far, far_obs)
        tri[0] = both[0]
        tri[1] = both[1]

    @pl.when(jnp.logical_not(kind_a))
    def _():
        first = pair_sums(own, own_obs, own, own_obs)
        second = pair_sums(mate, mate_obs, mate, mate_obs)
        diag = (first[0] + second[0], first[1] + second[1])

        @pl.when(lo == 0)
        def _():
            put(keep_a, send_a, diag)

        @pl.when(lo == 1)
        def _():
            put(send_a, keep_a, diag)

        both = pair_sums(far, far_obs, own, own_obs)
        tri[0] = both[0]
        tri[1] = both[1]


def ratio(num, den):
    return num / jnp.maximum(den, 1.0)


def ratio_kernel(role, half_sum, full_a, full_b, mirror_a, mirror_b, cut_a, cut_b, tri, tri_in, send, keep):
    par, lo, core = role[0], role[1], role[2]
    kind_a = core == par
    outer = lo == par
    even = par == 0

    def joined(first, second, i):
        return jnp.concatenate([first[i], second[i]], axis=1)

    @pl.when(kind_a & outer)
    def _():
        num = joined(mirror_a, mirror_b, 0) + joined(cut_a, cut_b, 0).T
        den = joined(mirror_a, mirror_b, 1) + joined(cut_a, cut_b, 1).T
        value = ratio(num, den)

        @pl.when(even)
        def _():
            keep[:, :128] = value[:, :128]
            send[:, :384] = value[:, 128:]

        @pl.when(jnp.logical_not(even))
        def _():
            keep[:, :128] = value[:, 384:]
            send[:, :384] = value[:, :384]

    @pl.when(kind_a & jnp.logical_not(outer))
    def _():
        num = joined(full_a, full_b, 0) + joined(mirror_a, mirror_b, 0).T
        den = joined(full_a, full_b, 1) + joined(mirror_a, mirror_b, 1).T
        value = ratio(num, den)
        beyond = ratio(tri[0] + tri_in[0], tri[1] + tri_in[1])

        @pl.when(even)
        def _():
            keep[:, :384] = value[:, :384]
            send[:, :128] = value[:, 384:]
            send[:, 128:] = beyond

        @pl.when(jnp.logical_not(even))
        def _():
            keep[:, :384] = value[:, 128:]
            send[:, 512:] = value[:, :128]
            send[:, :512] = beyond

    @pl.when(jnp.logical_not(kind_a) & outer)
    def _():
        send[:, :512] = ratio(tri[0] + tri_in[0], tri[1] + tri_in[1]).T
        keep[:, :256] = ratio(half_sum[0], half_sum[1])

    @pl.when(jnp.logical_not(kind_a) & jnp.logical_not(outer))
    def _():
        send[:, :256] = ratio(half_sum[0], half_sum[1])


def place_kernel(role, row_cohort, col_cohort, keep, came, out):
    par, lo, core = role[0], role[1], role[2]
    kind_a = core == par
    outer = lo == par
    rows = row_cohort[...]

    def put(start, value):
        width = value.shape[1]
        same = rows == col_cohort[:, start : start + width]
        out[:, start : start + width] = jnp.where(same, value, 0.0)

    def one(parity, far_kind, outer_kind, parts):
        want = (par == parity) & (kind_a == far_kind) & (outer == outer_kind)

        @pl.when(want)
        def _():
            start = 0
            for ref, width in parts:
                put(start, ref[:, :width])
                start += width

    one(0, True, True, [(came, 512), (keep, 128)])
    one(0, False, True, [(came, 384), (keep, 256)])
    one(0, True, False, [(came, 256), (keep, 384)])
    one(0, False, False, [(came, 640)])
    one(1, False, False, [(came, 640)])
    one(1, True, False, [(keep, 384), (came, 256)])
    one(1, False, True, [(keep, 256), (came, 384)])
    one(1, True, True, [(keep, 128), (came, 512)])


def cohort_of(positions, cohort_ends):
    return jnp.sum((cohort_ends[None, :] <= positions[:, None]).astype(jnp.int32), axis=1)


def call(kernel, out_shapes, in_count, scratch=()):
    vmem = pl.BlockSpec(memory_space=pltpu.VMEM)
    return pl.pallas_call(
        kernel,
        out_shape=out_shapes,
        in_specs=[pl.BlockSpec(memory_space=pltpu.SMEM)] + [vmem] * in_count,
        out_specs=jax.tree.map(lambda _: vmem, out_shapes),
        scratch_shapes=list(scratch),
        compiler_params=pltpu.CompilerParams(vmem_limit_bytes=50 * 1024 * 1024),
    )


def per_device(probs, cohort_sizes):
    blocks = lax.axis_size("cohort")
    block = lax.axis_index("cohort")
    quarter = lax.axis_index("variant")
    role = jnp.stack([block % 2, quarter // 2, quarter % 2]).astype(jnp.int32)

    def move(value, rule):
        return lax.ppermute(value, AXES, route(blocks, rule))

    mate = move(probs, to_mate)
    far = move(probs, to_next)
    half = jax.ShapeDtypeStruct((2, TILE, HALF), F32)
    full = jax.ShapeDtypeStruct((2, TILE, TILE), F32)
    obs = pltpu.VMEM(probs.shape[1:], jnp.bfloat16)
    send_a, send_b, keep_a, keep_b, tri = call(
        sums_kernel, (half, half, half, half, full), 3, (obs, obs, obs)
    )(role, probs, mate, far)
    full_a = keep_a + move(send_a, to_chip)
    tri = tri + move(tri, to_far)
    full_b = keep_b + move(send_b, to_chip_a)
    mirror_a = move(full_a, to_mirror)
    cut_a = move(full_a, to_cut)
    tri_in = move(tri, to_owner)
    mirror_b = move(full_b, to_mirror)
    cut_b = move(full_b, to_cut)
    wide = jax.ShapeDtypeStruct((TILE, WIDTH), F32)
    narrow = jax.ShapeDtypeStruct((TILE, 384), F32)
    send, keep = call(ratio_kernel, (wide, narrow), 9)(
        role, full_a, full_a, full_b, mirror_a, mirror_b, cut_a, cut_b, tri, tri_in
    )
    came = move(send, to_core)

    cohort_ends = jnp.cumsum(cohort_sizes)
    row_pos = block * TILE + jnp.arange(TILE, dtype=jnp.int32)
    col_pos = (block - 2) * TILE + quarter * WIDTH + jnp.arange(WIDTH, dtype=jnp.int32)
    inside = (col_pos >= 0) & (col_pos < TILE * blocks)
    row_cohort = cohort_of(row_pos, cohort_ends)[:, None]
    col_cohort = jnp.where(inside, cohort_of(col_pos, cohort_ends), -1)[None, :]
    return call(place_kernel, wide, 4)(role, row_cohort, col_cohort, keep, came)


def solution(mesh):
    return jax.shard_map(
        per_device,
        mesh=mesh,
        in_specs=(P(None, "cohort", "variant"), P()),
        out_specs=P("cohort", "variant"),
        check_vma=False,
    )
```

```python
import jax
import jax.numpy as jnp
from jax import lax
from jax.experimental import pallas as pl
from jax.experimental.pallas import tpu as pltpu
from jax.sharding import PartitionSpec as P

AXES = ("cohort", "variant")
TILE = 512
HALF = 256
WIDTH = 640
F32 = jnp.float32
VMEM = 24 * 1024 * 1024


def route(blocks, rule):
    pairs = []
    for k in range(blocks // 2):
        for par in range(2):
            for lo in range(2):
                for core in range(2):
                    to = rule(k, par, lo, core)
                    if to is not None and 0 <= to[0] < blocks // 2:
                        source = (2 * k + par) * 4 + lo * 2 + core
                        pairs.append((source, (2 * to[0] + to[1]) * 4 + to[2] * 2 + to[3]))
    return pairs


def is_a(par, core):
    return core == par


def is_outer(par, lo):
    return lo == par


def to_mate(k, par, lo, core):
    if is_a(par, core):
        return (k, par, lo, 1 - core)
    return (k, 1 - par, lo, core)


def to_next(k, par, lo, core):
    return (k - 1 if core == 0 else k + 1, par, lo, core)


def to_chip(k, par, lo, core):
    return (k, par, 1 - lo, core) if is_a(par, core) else None


def to_across(k, par, lo, core):
    return None if is_a(par, core) else (k, par, 1 - lo, 1 - core)


def to_side(k, par, lo, core):
    return None if is_a(par, core) else (k, par, lo, 1 - core)


def to_far(k, par, lo, core):
    if is_a(par, core):
        return None
    return (k + 1 if core == 0 else k - 1, par, lo, 1 - core)


def to_mirror(k, par, lo, core):
    return (k, 1 - par, 1 - lo, 1 - core) if is_a(par, core) else None


def to_cut(k, par, lo, core):
    if is_a(par, core) and is_outer(par, lo):
        return (k + 1 if par == 0 else k - 1, par, lo, core)
    return None


def to_core(k, par, lo, core):
    return (k, par, lo, 1 - core) if is_a(par, core) else None


def dot_t(left, right):
    return lax.dot_general(left, right, (((1,), (1,)), ((), ())), preferred_element_type=F32)


def observed(data):
    total = data[0].astype(F32) + data[1].astype(F32) + data[2].astype(F32)
    return total.astype(jnp.bfloat16)


def pair_sums(left, left_obs, right, right_obs):
    cross = dot_t(left[0], right[2]) + dot_t(left[2], right[0])
    num = dot_t(left[1], right[1]) - 2.0 * cross
    den = dot_t(left[1], right_obs) + dot_t(left_obs, right[1])
    return num, den


def put_rows(first, second, values, swap):
    @pl.when(swap)
    def _():
        for i in range(2):
            first[i] = values[i][HALF:]
            second[i] = values[i][:HALF]

    @pl.when(jnp.logical_not(swap))
    def _():
        for i in range(2):
            first[i] = values[i][:HALF]
            second[i] = values[i][HALF:]


def put_tiles(tri, values, par, beyond):
    def put(parity, reach, first, second):
        @pl.when((par == parity) & (beyond == reach))
        def _():
            for i in range(2):
                tri[i, :HALF] = values[i][first]
                tri[i, HALF:] = values[i][second]

    low, high = slice(0, HALF), slice(HALF, TILE)
    put(0, 1, (high, low), (high, high))
    put(0, 0, (high, low), (low, low))
    put(1, 1, (low, high), (low, low))
    put(1, 0, (low, high), (high, high))


def fetch(source, target, sems, order=(1, 0, 2)):
    for plane in order:
        pltpu.make_async_copy(source.at[plane], target.at[plane], sems.at[plane]).start()


def arrived(source, target, sems, plane):
    pltpu.make_async_copy(source.at[plane], target.at[plane], sems.at[plane]).wait()


def first_kernel(role, own, mate, far, send_a, send_b, tri, left, right, left_sems, right_sems):
    par, lo, core, beyond = role[0], role[1], role[2], role[3]
    kind_a = core == par
    outer = lo == par

    @pl.when(kind_a & outer)
    def _():
        fetch(own, left, left_sems)
        fetch(mate, right, right_sems, (1, 2, 0))

    @pl.when(kind_a & jnp.logical_not(outer))
    def _():
        fetch(far, left, left_sems)
        fetch(mate, right, right_sems, (1, 2, 0))

    @pl.when(jnp.logical_not(kind_a))
    def _():
        fetch(far, left, left_sems)
        fetch(own, right, right_sems, (1, 2, 0))

    arrived(own, left, left_sems, 1)
    arrived(own, right, right_sems, 1)
    same = dot_t(left[1], right[1])
    arrived(own, left, left_sems, 0)
    arrived(own, right, right_sems, 2)
    cross = dot_t(left[0], right[2])
    arrived(own, left, left_sems, 2)
    arrived(own, right, right_sems, 0)
    cross = cross + dot_t(left[2], right[0])
    den = dot_t(left[1], observed(right)) + dot_t(observed(left), right[1])
    values = (same - 2.0 * cross, den)

    @pl.when(kind_a)
    def _():
        put_rows(send_a, send_b, values, outer == (par == 0))

    @pl.when(jnp.logical_not(kind_a))
    def _():
        put_tiles(tri, values, par, beyond)


def second_kernel(role, own, mate, far, keep_a, keep_b, tri, send_d, keep_d, own_v, mate_v, far_v, sems):
    par, lo, core, beyond = role[0], role[1], role[2], role[3]
    kind_a = core == par
    outer = lo == par

    def ready(source, target, which):
        for plane in (1, 0, 2):
            arrived(source, target, sems.at[which], plane)

    fetch(own, own_v, sems.at[0])

    @pl.when(kind_a)
    def _():
        fetch(far, far_v, sems.at[2])

    fetch(mate, mate_v, sems.at[1])
    ready(own, own_v, 0)
    own_obs = observed(own_v)

    @pl.when(kind_a)
    def _():
        ready(far, far_v, 2)
        far_obs = observed(far_v)
        put_tiles(tri, pair_sums(own_v, own_obs, far_v, far_obs), par, beyond)
        ready(mate, mate_v, 1)
        mate_obs = observed(mate_v)

        @pl.when(outer)
        def _():
            put_rows(keep_a, keep_b, pair_sums(far_v, far_obs, mate_v, mate_obs), par == 1)

        @pl.when(jnp.logical_not(outer))
        def _():
            put_rows(keep_a, keep_b, pair_sums(own_v, own_obs, mate_v, mate_obs), par == 0)

    @pl.when(jnp.logical_not(kind_a))
    def _():
        first = pair_sums(own_v, own_obs, own_v, own_obs)
        ready(mate, mate_v, 1)
        mate_obs = observed(mate_v)
        second = pair_sums(mate_v, mate_obs, mate_v, mate_obs)
        diag = (first[0] + second[0], first[1] + second[1])

        @pl.when(lo == 0)
        def _():
            for i in range(2):
                keep_d[i] = diag[i][:, :HALF]
                send_d[i] = diag[i][:, HALF:]

        @pl.when(lo == 1)
        def _():
            for i in range(2):
                send_d[i] = diag[i][:, :HALF]
                keep_d[i] = diag[i][:, HALF:]


def merge_kernel(role, held, kept, tri, tri_in, send, keep):
    par, lo, core = role[0], role[1], role[2]
    outer = lo == par
    row = lax.broadcasted_iota(jnp.int32, (HALF, HALF), 0)

    def near(source, target):
        first = jnp.where(par == 0, 0, HALF - role[5])
        free = (row >= first) & (row < first + role[5])
        for i in range(2):
            tile = (tri[i, :HALF] + tri_in[i, :HALF]).T
            other = (tri[i, HALF:] + tri_in[i, HALF:]).T

            @pl.when(par == 0)
            def _():
                target[i, :, HALF:] = jnp.where(free, tile, source[i, :, HALF:])
                target[i, :, :HALF] = jnp.where(free, other, source[i, :, :HALF])

            @pl.when(par == 1)
            def _():
                target[i, :, :HALF] = jnp.where(free, tile, source[i, :, :HALF])
                target[i, :, HALF:] = jnp.where(free, other, source[i, :, HALF:])

    def across(source, target):
        first = jnp.where(par == 0, HALF - role[6], 0)
        free = (row >= first) & (row < first + role[6])
        for i in range(2):
            tile = tri[i, :HALF] + tri_in[i, :HALF]
            other = tri[i, HALF:] + tri_in[i, HALF:]

            @pl.when(par == 0)
            def _():
                target[i, :, :HALF] = jnp.where(free, tile, source[i, :, :HALF])
                target[i, :, HALF:] = jnp.where(free, other, source[i, :, HALF:])

            @pl.when(par == 1)
            def _():
                target[i, :, HALF:] = jnp.where(free, tile, source[i, :, HALF:])
                target[i, :, :HALF] = jnp.where(free, other, source[i, :, :HALF])

    @pl.when((core == par) & outer)
    def _():
        near(held, send)
        across(kept, keep)

    @pl.when((core == par) & jnp.logical_not(outer))
    def _():
        across(held, send)
        near(kept, keep)


def ratio(num, den):
    return num / jnp.maximum(den, 1.0)


def ratio_kernel(role, full_a, full_b, mirror_a, mirror_b, cut_a, cut_b, diag, diag_in, send, keep):
    par, lo, core, beyond = role[0], role[1], role[2], role[4]
    kind_a = core == par
    outer = lo == par

    def ordered(first, second, i, swap):
        pair = (second[i], first[i]) if swap else (first[i], second[i])
        return jnp.concatenate(pair, axis=0)

    def behind(parity):
        flip = parity == 1
        num, den = [
            ordered(cut_a, cut_b, i, flip) + ordered(mirror_a, mirror_b, i, not flip).T
            for i in range(2)
        ]
        return ratio(num, den)

    def ahead(parity):
        flip = parity == 0
        num, den = [
            ordered(full_a, full_b, i, flip) + ordered(mirror_a, mirror_b, i, not flip).T
            for i in range(2)
        ]
        return ratio(num, den)

    def put_diag(target, start):
        target[:, start : start + HALF] = ratio(diag[0] + diag_in[0], diag[1] + diag_in[1])

    def put_tiles_at(target, start, parity, source, flip):
        near_x = HALF if parity == 0 else 0
        near_z = HALF - near_x
        both = near_z if flip else near_x
        first, second = [
            ratio(source[0, :, at : at + HALF], source[1, :, at : at + HALF]).T
            for at in (both, HALF - both)
        ]

        def place(x, z, value):
            row, col = (z, x) if flip else (x, z)
            target[row : row + HALF, start + col : start + col + HALF] = value

        zero = jnp.zeros((HALF, HALF), F32)
        place(near_x, near_z, first)
        place(HALF - near_x, HALF - near_z, zero)

        @pl.when(beyond == 1)
        def _():
            place(near_x, HALF - near_z, second)
            place(HALF - near_x, near_z, zero)

        @pl.when(beyond == 0)
        def _():
            place(HALF - near_x, near_z, second)
            place(near_x, HALF - near_z, zero)

    def when(parity, want_outer):
        return pl.when((par == parity) & kind_a & (outer == want_outer))

    @when(0, True)
    def _():
        value = behind(0)
        put_tiles_at(keep, 0, 0, cut_b, True)
        keep[:, 512:] = value[:, :128]
        send[:, :384] = value[:, 128:]
        put_diag(send, 384)

    @when(1, True)
    def _():
        value = behind(1)
        keep[:, :128] = value[:, 384:]
        put_tiles_at(keep, 128, 1, cut_b, True)
        put_diag(send, 0)
        send[:, 256:] = value[:, :384]

    @when(0, False)
    def _():
        value = ahead(0)
        put_diag(keep, 0)
        keep[:, 256:] = value[:, :384]
        send[:, :128] = value[:, 384:]
        put_tiles_at(send, 128, 0, full_b, False)

    @when(1, False)
    def _():
        value = ahead(1)
        put_tiles_at(send, 0, 1, full_b, False)
        send[:, 512:] = value[:, :128]
        keep[:, :384] = value[:, 128:]
        put_diag(keep, 384)


def place_kernel(role, row_cohort, col_cohort, keep, came, out):
    same = row_cohort[...] == col_cohort[...]

    @pl.when(role[2] == role[0])
    def _():
        out[...] = jnp.where(same, keep[...], 0.0)

    @pl.when(role[2] != role[0])
    def _():
        out[...] = jnp.where(same, came[...], 0.0)


def cohort_of(positions, cohort_ends):
    return jnp.sum((cohort_ends[None, :] <= positions[:, None]).astype(jnp.int32), axis=1)


def call(kernel, out_shapes, in_count, scratch=(), space=pltpu.VMEM):
    vmem = pl.BlockSpec(memory_space=pltpu.VMEM)
    return pl.pallas_call(
        kernel,
        out_shape=out_shapes,
        in_specs=[pl.BlockSpec(memory_space=pltpu.SMEM)] + [pl.BlockSpec(memory_space=space)] * in_count,
        out_specs=jax.tree.map(lambda _: vmem, out_shapes),
        scratch_shapes=list(scratch),
        compiler_params=pltpu.CompilerParams(vmem_limit_bytes=VMEM),
    )


def per_device(probs, cohort_sizes):
    blocks = lax.axis_size("cohort")
    block = lax.axis_index("cohort")
    quarter = lax.axis_index("variant")
    par, lo, core = block % 2, quarter // 2, quarter % 2
    kind_a = core == par
    outer = lo == par
    cohort_ends = jnp.cumsum(cohort_sizes)

    def cohorts(start):
        position = start * TILE + jnp.arange(TILE, dtype=jnp.int32)
        return jnp.where(position < 0, -1, cohort_of(position, cohort_ends))

    step = jnp.where(par == 0, 2, -2)
    own_ids, ahead_ids, back_ids = cohorts(block), cohorts(block + step), cohorts(block - step)
    even = par == 0

    def split(ids, low):
        low_half, high_half = ids[:HALF], ids[HALF:]
        return jnp.where(low, low_half, high_half), jnp.where(low, high_half, low_half)

    def reach(x_ids, z_ids):
        x_near, _ = split(x_ids, jnp.logical_not(even))
        z_near, z_far = split(z_ids, even)
        x_edge = jnp.where(even, x_ids[-1], x_ids[0])
        z_edge = jnp.where(even, z_ids[0], z_ids[-1])
        beyond = jnp.any(z_far == x_edge)
        return jnp.sum(z_near == x_edge), jnp.sum(x_near == z_edge), beyond

    z_count, x_count, beyond_ahead = reach(own_ids, ahead_ids)
    _, _, beyond_back = reach(back_ids, own_ids)
    role = jnp.stack(
        [
            par,
            lo,
            core,
            jnp.where(kind_a, beyond_ahead, beyond_back),
            jnp.where(outer, beyond_back, beyond_ahead),
            z_count,
            x_count,
        ]
    ).astype(jnp.int32)

    def move(value, rule):
        return lax.ppermute(value, AXES, route(blocks, rule))

    mate = move(probs, to_mate)
    far = move(probs, to_next)
    half = jax.ShapeDtypeStruct((2, TILE, HALF), F32)
    rows = jax.ShapeDtypeStruct((2, HALF, TILE), F32)
    block_of = pltpu.VMEM(probs.shape, probs.dtype)
    planes = pltpu.SemaphoreType.DMA((3,))
    send_a, held_b, send_t = call(
        first_kernel, (rows, rows, half), 3, (block_of, block_of, planes, planes), pltpu.HBM
    )(role, probs, mate, far)
    came_a = move(send_a, to_chip)
    tri_in = move(send_t, to_far)
    keep_a, kept_b, tri, send_d, keep_d = call(
        second_kernel,
        (rows, rows, half, half, half),
        3,
        (block_of, block_of, block_of, pltpu.SemaphoreType.DMA((3, 3))),
        pltpu.HBM,
    )(role, probs, mate, far)
    send_b, keep_b = call(merge_kernel, (rows, rows), 4)(role, held_b, kept_b, tri, tri_in)
    came_b = move(send_b, to_chip)
    full_a = keep_a + came_a
    mirror_a = move(full_a, to_mirror)
    cut_a = move(full_a, to_cut)
    send_d, keep_d, came_b = lax.optimization_barrier((send_d, keep_d, came_b))
    full_b = keep_b + came_b
    mirror_b = move(full_b, to_mirror)
    cut_b = move(full_b, to_cut)
    diag_in = move(send_d, to_across)
    diag = move(keep_d, to_side)
    wide = jax.ShapeDtypeStruct((TILE, WIDTH), F32)
    send, keep = call(ratio_kernel, (wide, wide), 8)(
        role, full_a, full_b, mirror_a, mirror_b, cut_a, cut_b, diag, diag_in
    )
    came = move(send, to_core)

    col_pos = (block - 2) * TILE + quarter * WIDTH + jnp.arange(WIDTH, dtype=jnp.int32)
    inside = (col_pos >= 0) & (col_pos < TILE * blocks)
    row_cohort = own_ids[:, None]
    col_cohort = jnp.where(inside, cohort_of(col_pos, cohort_ends), -1)[None, :]
    return call(place_kernel, wide, 4)(role, row_cohort, col_cohort, keep, came)


def solution(mesh):
    return jax.shard_map(
        per_device,
        mesh=mesh,
        in_specs=(P(None, "cohort", "variant"), P()),
        out_specs=P("cohort", "variant"),
        check_vma=False,
    )
```

```python
import jax
import jax.numpy as jnp
from jax import lax
from jax.experimental import pallas as pl
from jax.experimental.pallas import tpu as pltpu
from jax.sharding import PartitionSpec as P

AXES = ("cohort", "variant")
TILE = 512
HALF = 256
WIDTH = 640
F32 = jnp.float32
VMEM = 24 * 1024 * 1024


def route(blocks, rule):
    pairs = []
    for k in range(blocks // 2):
        for par in range(2):
            for lo in range(2):
                for core in range(2):
                    to = rule(k, par, lo, core)
                    if to is not None and 0 <= to[0] < blocks // 2:
                        source = (2 * k + par) * 4 + lo * 2 + core
                        pairs.append((source, (2 * to[0] + to[1]) * 4 + to[2] * 2 + to[3]))
    return pairs


def is_a(par, core):
    return core == par


def is_outer(par, lo):
    return lo == par


def to_mate(k, par, lo, core):
    if is_a(par, core):
        return (k, par, lo, 1 - core)
    return (k, 1 - par, lo, core)


def to_next(k, par, lo, core):
    return (k - 1 if core == 0 else k + 1, par, lo, core)


def to_chip(k, par, lo, core):
    return (k, par, 1 - lo, core) if is_a(par, core) else None


def to_across(k, par, lo, core):
    return None if is_a(par, core) else (k, par, 1 - lo, 1 - core)


def to_side(k, par, lo, core):
    return None if is_a(par, core) else (k, par, lo, 1 - core)


def to_far(k, par, lo, core):
    if is_a(par, core):
        return None
    return (k + 1 if core == 0 else k - 1, par, lo, 1 - core)


def to_mirror(k, par, lo, core):
    return (k, 1 - par, 1 - lo, 1 - core) if is_a(par, core) else None


def to_cut(k, par, lo, core):
    if is_a(par, core) and is_outer(par, lo):
        return (k + 1 if par == 0 else k - 1, par, lo, core)
    return None


def to_core(k, par, lo, core):
    return (k, par, lo, 1 - core) if is_a(par, core) else None


def dot_t(left, right):
    return lax.dot_general(left, right, (((1,), (1,)), ((), ())), preferred_element_type=F32)


def observed(data):
    total = data[0].astype(F32) + data[1].astype(F32) + data[2].astype(F32)
    return total.astype(jnp.bfloat16)


def pair_sums(left, left_obs, right, right_obs):
    cross = dot_t(left[0], right[2]) + dot_t(left[2], right[0])
    num = dot_t(left[1], right[1]) - 2.0 * cross
    den = dot_t(left[1], right_obs) + dot_t(left_obs, right[1])
    return num, den


def put_rows(first, second, values, swap):
    @pl.when(swap)
    def _():
        for i in range(2):
            first[i] = values[i][HALF:]
            second[i] = values[i][:HALF]

    @pl.when(jnp.logical_not(swap))
    def _():
        for i in range(2):
            first[i] = values[i][:HALF]
            second[i] = values[i][HALF:]


def put_tiles(tri, left, right, par, beyond):
    near_left = jnp.where(par == 0, HALF, 0)
    near_right = HALF - near_left
    other_left = jnp.where(beyond == 1, near_left, near_right)
    other_right = jnp.where(beyond == 1, near_left, near_right)

    def rows(data, start):
        at = pl.ds(pl.multiple_of(start, HALF), HALF)
        return [data[plane, at, :] for plane in range(3)]

    for tile, (l, r) in enumerate(((near_left, near_right), (other_left, other_right))):
        left_rows, right_rows = rows(left, l), rows(right, r)
        num, den = pair_sums(left_rows, observed(left_rows), right_rows, observed(right_rows))
        tri[0, tile * HALF : (tile + 1) * HALF] = num
        tri[1, tile * HALF : (tile + 1) * HALF] = den


def fetch(source, target, sems, order=(1, 0, 2)):
    for plane in order:
        pltpu.make_async_copy(source.at[plane], target.at[plane], sems.at[plane]).start()


def arrived(source, target, sems, plane):
    pltpu.make_async_copy(source.at[plane], target.at[plane], sems.at[plane]).wait()


def stage_kernel(role, own, out, out_obs):
    out[...] = own[...]
    out_obs[...] = observed(own)


def tiles_kernel(role, own, far, tri, far_v, sems):
    par, core, beyond = role[0], role[2], role[3]

    @pl.when(core != par)
    def _():
        fetch(far, far_v, sems)
        for plane in range(3):
            arrived(far, far_v, sems, plane)
        put_tiles(tri, far_v, own, par, beyond)


def first_kernel(role, own, own_obs, mate, far, after, send_a, send_b, far_v, sems):
    par, lo, core = role[0], role[1], role[2]
    kind_a = core == par
    outer = lo == par

    @pl.when(kind_a & outer)
    def _():
        put_rows(send_a, send_b, pair_sums(own, own_obs[...], mate, observed(mate)), par == 0)

    @pl.when(kind_a & jnp.logical_not(outer))
    def _():
        fetch(far, far_v, sems)
        mate_obs = observed(mate)
        arrived(far, far_v, sems, 1)
        same = dot_t(far_v[1], mate[1])
        den = dot_t(far_v[1], mate_obs)
        arrived(far, far_v, sems, 0)
        cross = dot_t(far_v[0], mate[2])
        arrived(far, far_v, sems, 2)
        cross = cross + dot_t(far_v[2], mate[0])
        den = den + dot_t(observed(far_v), mate[1])
        put_rows(send_a, send_b, (same - 2.0 * cross, den), par == 1)


def second_kernel(role, own, own_obs, mate, far, keep_a, keep_b, tri, send_d, keep_d, far_v, sems):
    par, lo, core, beyond = role[0], role[1], role[2], role[3]
    outer = lo == par

    @pl.when(core == par)
    def _():
        fetch(far, far_v, sems)
        for plane in range(3):
            arrived(far, far_v, sems, plane)
        put_tiles(tri, own, far_v, par, beyond)

        @pl.when(outer)
        def _():
            put_rows(keep_a, keep_b, pair_sums(far_v, observed(far_v), mate, observed(mate)), par == 1)

        @pl.when(jnp.logical_not(outer))
        def _():
            put_rows(keep_a, keep_b, pair_sums(own, own_obs[...], mate, observed(mate)), par == 0)

    @pl.when(core != par)
    def _():
        first = pair_sums(own, own_obs[...], own, own_obs[...])
        mate_obs = observed(mate)
        second = pair_sums(mate, mate_obs, mate, mate_obs)
        diag = (first[0] + second[0], first[1] + second[1])

        @pl.when(lo == 0)
        def _():
            for i in range(2):
                keep_d[i] = diag[i][:, :HALF]
                send_d[i] = diag[i][:, HALF:]

        @pl.when(lo == 1)
        def _():
            for i in range(2):
                send_d[i] = diag[i][:, :HALF]
                keep_d[i] = diag[i][:, HALF:]


def merge_kernel(role, held, kept, tri, tri_in, send, keep):
    par, lo, core = role[0], role[1], role[2]
    outer = lo == par
    row = lax.broadcasted_iota(jnp.int32, (HALF, HALF), 0)

    def near(source, target):
        first = jnp.where(par == 0, 0, HALF - role[5])
        free = (row >= first) & (row < first + role[5])
        for i in range(2):
            tile = (tri[i, :HALF] + tri_in[i, :HALF]).T
            other = (tri[i, HALF:] + tri_in[i, HALF:]).T

            @pl.when(par == 0)
            def _():
                target[i, :, HALF:] = jnp.where(free, tile, source[i, :, HALF:])
                target[i, :, :HALF] = jnp.where(free, other, source[i, :, :HALF])

            @pl.when(par == 1)
            def _():
                target[i, :, :HALF] = jnp.where(free, tile, source[i, :, :HALF])
                target[i, :, HALF:] = jnp.where(free, other, source[i, :, HALF:])

    def across(source, target):
        first = jnp.where(par == 0, HALF - role[6], 0)
        free = (row >= first) & (row < first + role[6])
        for i in range(2):
            tile = tri[i, :HALF] + tri_in[i, :HALF]
            other = tri[i, HALF:] + tri_in[i, HALF:]

            @pl.when(par == 0)
            def _():
                target[i, :, :HALF] = jnp.where(free, tile, source[i, :, :HALF])
                target[i, :, HALF:] = jnp.where(free, other, source[i, :, HALF:])

            @pl.when(par == 1)
            def _():
                target[i, :, HALF:] = jnp.where(free, tile, source[i, :, HALF:])
                target[i, :, :HALF] = jnp.where(free, other, source[i, :, :HALF])

    @pl.when((core == par) & outer)
    def _():
        near(held, send)
        across(kept, keep)

    @pl.when((core == par) & jnp.logical_not(outer))
    def _():
        across(held, send)
        near(kept, keep)


def ratio(num, den):
    return num / jnp.maximum(den, 1.0)


def ratio_kernel(role, diag_in, diag, cut_a, cut_b, mirror_a, mirror_b, full_a, full_b, send, keep):
    par, lo, core, beyond = role[0], role[1], role[2], role[4]
    kind_a = core == par
    outer = lo == par

    def ordered(first, second, i, swap):
        pair = (second[i], first[i]) if swap else (first[i], second[i])
        return jnp.concatenate(pair, axis=0)

    def behind(parity):
        flip = parity == 1
        num, den = [
            ordered(cut_a, cut_b, i, flip) + ordered(mirror_a, mirror_b, i, not flip).T
            for i in range(2)
        ]
        return ratio(num, den)

    def ahead(parity):
        flip = parity == 0
        num, den = [
            ordered(full_a, full_b, i, flip) + ordered(mirror_a, mirror_b, i, not flip).T
            for i in range(2)
        ]
        return ratio(num, den)

    def put_diag(target, start):
        target[:, start : start + HALF] = ratio(diag[0] + diag_in[0], diag[1] + diag_in[1])

    def put_tiles_at(target, start, parity, source, flip):
        near_x = HALF if parity == 0 else 0
        near_z = HALF - near_x
        both = near_z if flip else near_x
        first, second = [
            ratio(source[0, :, at : at + HALF], source[1, :, at : at + HALF]).T
            for at in (both, HALF - both)
        ]

        def place(x, z, value):
            row, col = (z, x) if flip else (x, z)
            target[row : row + HALF, start + col : start + col + HALF] = value

        zero = jnp.zeros((HALF, HALF), F32)
        place(near_x, near_z, first)
        place(HALF - near_x, HALF - near_z, zero)

        @pl.when(beyond == 1)
        def _():
            place(near_x, HALF - near_z, second)
            place(HALF - near_x, near_z, zero)

        @pl.when(beyond == 0)
        def _():
            place(HALF - near_x, near_z, second)
            place(near_x, HALF - near_z, zero)

    def when(parity, want_outer):
        return pl.when((par == parity) & kind_a & (outer == want_outer))

    @when(0, True)
    def _():
        value = behind(0)
        put_tiles_at(keep, 0, 0, cut_b, True)
        keep[:, 512:] = value[:, :128]
        send[:, :384] = value[:, 128:]
        put_diag(send, 384)

    @when(1, True)
    def _():
        value = behind(1)
        keep[:, :128] = value[:, 384:]
        put_tiles_at(keep, 128, 1, cut_b, True)
        put_diag(send, 0)
        send[:, 256:] = value[:, :384]

    @when(0, False)
    def _():
        value = ahead(0)
        put_diag(keep, 0)
        keep[:, 256:] = value[:, :384]
        send[:, :128] = value[:, 384:]
        put_tiles_at(send, 128, 0, full_b, False)

    @when(1, False)
    def _():
        value = ahead(1)
        put_tiles_at(send, 0, 1, full_b, False)
        send[:, 512:] = value[:, :128]
        keep[:, :384] = value[:, 128:]
        put_diag(keep, 384)


def place_kernel(role, row_cohort, col_cohort, keep, came, out):
    same = row_cohort[...] == col_cohort[...]

    @pl.when(role[2] == role[0])
    def _():
        out[...] = jnp.where(same, keep[...], 0.0)

    @pl.when(role[2] != role[0])
    def _():
        out[...] = jnp.where(same, came[...], 0.0)


def cohort_of(positions, cohort_ends):
    return jnp.sum((cohort_ends[None, :] <= positions[:, None]).astype(jnp.int32), axis=1)


def call(kernel, out_shapes, spaces, scratch=()):
    vmem = pl.BlockSpec(memory_space=pltpu.VMEM)
    return pl.pallas_call(
        kernel,
        out_shape=out_shapes,
        in_specs=[pl.BlockSpec(memory_space=pltpu.SMEM)] + [pl.BlockSpec(memory_space=space) for space in spaces],
        out_specs=jax.tree.map(lambda _: vmem, out_shapes),
        scratch_shapes=list(scratch),
        compiler_params=pltpu.CompilerParams(vmem_limit_bytes=VMEM),
    )


def per_device(probs, cohort_sizes):
    blocks = lax.axis_size("cohort")
    block = lax.axis_index("cohort")
    quarter = lax.axis_index("variant")
    par, lo, core = block % 2, quarter // 2, quarter % 2
    kind_a = core == par
    outer = lo == par
    cohort_ends = jnp.cumsum(cohort_sizes)

    def cohorts(start):
        position = start * TILE + jnp.arange(TILE, dtype=jnp.int32)
        return jnp.where(position < 0, -1, cohort_of(position, cohort_ends))

    step = jnp.where(par == 0, 2, -2)
    own_ids, ahead_ids, back_ids = cohorts(block), cohorts(block + step), cohorts(block - step)
    even = par == 0

    def split(ids, low):
        low_half, high_half = ids[:HALF], ids[HALF:]
        return jnp.where(low, low_half, high_half), jnp.where(low, high_half, low_half)

    def reach(x_ids, z_ids):
        x_near, _ = split(x_ids, jnp.logical_not(even))
        z_near, z_far = split(z_ids, even)
        x_edge = jnp.where(even, x_ids[-1], x_ids[0])
        z_edge = jnp.where(even, z_ids[0], z_ids[-1])
        beyond = jnp.any(z_far == x_edge)
        return jnp.sum(z_near == x_edge), jnp.sum(x_near == z_edge), beyond

    z_count, x_count, beyond_ahead = reach(own_ids, ahead_ids)
    _, _, beyond_back = reach(back_ids, own_ids)
    role = jnp.stack(
        [
            par,
            lo,
            core,
            jnp.where(kind_a, beyond_ahead, beyond_back),
            jnp.where(outer, beyond_back, beyond_ahead),
            z_count,
            x_count,
        ]
    ).astype(jnp.int32)

    def move(value, rule):
        return lax.ppermute(value, AXES, route(blocks, rule))

    far = move(probs, to_next)
    mate = move(probs, to_mate)
    half = jax.ShapeDtypeStruct((2, TILE, HALF), F32)
    rows = jax.ShapeDtypeStruct((2, HALF, TILE), F32)
    block_of = pltpu.VMEM(probs.shape, probs.dtype)
    planes = pltpu.SemaphoreType.DMA((3,))
    obs = jax.ShapeDtypeStruct(probs.shape[1:], probs.dtype)
    vmem = pltpu.VMEM
    own, own_obs = call(stage_kernel, (jax.ShapeDtypeStruct(probs.shape, probs.dtype), obs), [vmem])(
        role, probs
    )
    send_t = call(tiles_kernel, half, (vmem, pl.ANY), (block_of, planes))(role, own, far)
    send_a, held_b = call(
        first_kernel, (rows, rows), (vmem, vmem, vmem, pl.ANY, pl.ANY), (block_of, planes)
    )(role, own, own_obs, mate, far, send_t)
    tri_in = move(send_t, to_far)
    came_a = move(send_a, to_chip)
    keep_a, kept_b, tri, send_d, keep_d = call(
        second_kernel,
        (rows, rows, half, half, half),
        (vmem, vmem, vmem, pl.ANY),
        (block_of, planes),
    )(role, own, own_obs, mate, far)
    send_b, keep_b = call(merge_kernel, (rows, rows), [pltpu.VMEM] * 4)(role, held_b, kept_b, tri, tri_in)
    came_b = move(send_b, to_chip)
    full_a = keep_a + came_a
    mirror_a = move(full_a, to_mirror)
    cut_a = move(full_a, to_cut)
    send_d, keep_d, came_b = lax.optimization_barrier((send_d, keep_d, came_b))
    diag_in = move(send_d, to_across)
    full_b = keep_b + came_b
    cut_b = move(full_b, to_cut)
    mirror_b = move(full_b, to_mirror)
    diag = move(keep_d, to_side)
    wide = jax.ShapeDtypeStruct((TILE, WIDTH), F32)
    send, keep = call(ratio_kernel, (wide, wide), [pltpu.VMEM] * 8)(
        role, diag_in, diag, cut_a, cut_b, mirror_a, mirror_b, full_a, full_b
    )
    came = move(send, to_core)

    col_pos = (block - 2) * TILE + quarter * WIDTH + jnp.arange(WIDTH, dtype=jnp.int32)
    inside = (col_pos >= 0) & (col_pos < TILE * blocks)
    row_cohort = own_ids[:, None]
    col_cohort = jnp.where(inside, cohort_of(col_pos, cohort_ends), -1)[None, :]
    return call(place_kernel, wide, [pltpu.VMEM] * 4)(role, row_cohort, col_cohort, keep, came)


def solution(mesh):
    return jax.shard_map(
        per_device,
        mesh=mesh,
        in_specs=(P(None, "cohort", "variant"), P()),
        out_specs=P("cohort", "variant"),
        check_vma=False,
    )
```

```python
import jax
import jax.numpy as jnp
from jax import lax
from jax.experimental import pallas as pl
from jax.experimental.pallas import tpu as pltpu
from jax.sharding import PartitionSpec as P

AXES = ("cohort", "variant")
TILE = 512
HALF = 256
WIDTH = 640
F32 = jnp.float32
VMEM = 24 * 1024 * 1024


def route(blocks, rule):
    pairs = []
    for k in range(blocks // 2):
        for par in range(2):
            for lo in range(2):
                for core in range(2):
                    to = rule(k, par, lo, core)
                    if to is not None and 0 <= to[0] < blocks // 2:
                        source = (2 * k + par) * 4 + lo * 2 + core
                        pairs.append((source, (2 * to[0] + to[1]) * 4 + to[2] * 2 + to[3]))
    return pairs


def is_a(par, core):
    return core == par


def is_outer(par, lo):
    return lo == par


def to_mate(k, par, lo, core):
    if is_a(par, core):
        return (k, par, lo, 1 - core)
    return (k, 1 - par, lo, core)


def to_next(k, par, lo, core):
    return (k - 1 if core == 0 else k + 1, par, lo, core)


def to_chip(k, par, lo, core):
    return (k, par, 1 - lo, core) if is_a(par, core) else None


def to_across(k, par, lo, core):
    return None if is_a(par, core) else (k, par, 1 - lo, 1 - core)


def to_side(k, par, lo, core):
    return None if is_a(par, core) else (k, par, lo, 1 - core)


def to_far(k, par, lo, core):
    if is_a(par, core):
        return None
    return (k + 1 if core == 0 else k - 1, par, lo, 1 - core)


def to_mirror(k, par, lo, core):
    return (k, 1 - par, 1 - lo, 1 - core) if is_a(par, core) else None


def to_cut(k, par, lo, core):
    if is_a(par, core) and is_outer(par, lo):
        return (k + 1 if par == 0 else k - 1, par, lo, core)
    return None


def to_core(k, par, lo, core):
    return (k, par, lo, 1 - core) if is_a(par, core) else None


def dot_t(left, right):
    return lax.dot_general(left, right, (((1,), (1,)), ((), ())), preferred_element_type=F32)


def observed(data):
    total = data[0].astype(F32) + data[1].astype(F32) + data[2].astype(F32)
    return total.astype(jnp.bfloat16)


def pair_sums(left, left_obs, right, right_obs):
    cross = dot_t(left[0], right[2]) + dot_t(left[2], right[0])
    num = dot_t(left[1], right[1]) - 2.0 * cross
    den = dot_t(left[1], right_obs) + dot_t(left_obs, right[1])
    return num, den


def put_rows(first, second, values, swap):
    @pl.when(swap)
    def _():
        for i in range(2):
            first[i] = values[i][HALF:]
            second[i] = values[i][:HALF]

    @pl.when(jnp.logical_not(swap))
    def _():
        for i in range(2):
            first[i] = values[i][:HALF]
            second[i] = values[i][HALF:]


def put_tiles(tri, left, right, par, beyond):
    near_left = jnp.where(par == 0, HALF, 0)
    near_right = HALF - near_left
    other_left = jnp.where(beyond == 1, near_left, near_right)
    other_right = jnp.where(beyond == 1, near_left, near_right)

    def rows(data, start):
        at = pl.ds(pl.multiple_of(start, HALF), HALF)
        return [data[plane, at, :] for plane in range(3)]

    for tile, (l, r) in enumerate(((near_left, near_right), (other_left, other_right))):
        left_rows, right_rows = rows(left, l), rows(right, r)
        num, den = pair_sums(left_rows, observed(left_rows), right_rows, observed(right_rows))
        tri[0, tile * HALF : (tile + 1) * HALF] = num
        tri[1, tile * HALF : (tile + 1) * HALF] = den


def fetch(source, target, sems, order=(1, 0, 2)):
    for plane in order:
        pltpu.make_async_copy(source.at[plane], target.at[plane], sems.at[plane]).start()


def arrived(source, target, sems, plane):
    pltpu.make_async_copy(source.at[plane], target.at[plane], sems.at[plane]).wait()


def stage_kernel(role, own, out, out_obs):
    out[...] = own[...]
    out_obs[...] = observed(own)


def tiles_kernel(role, own, far, tri, far_v, sems):
    par, core, beyond = role[0], role[2], role[3]

    @pl.when(core != par)
    def _():
        fetch(far, far_v, sems)
        for plane in range(3):
            arrived(far, far_v, sems, plane)
        put_tiles(tri, far_v, own, par, beyond)


def chunk(data, start):
    at = pl.ds(pl.multiple_of(start, HALF), HALF)
    return [data[plane, at, :] for plane in range(3)]


def first_kernel(role, own, own_obs, mate, far, after, send_a, mate_obs, far_v, sems):
    par, lo, core = role[0], role[1], role[2]
    kind_a = core == par
    outer = lo == par
    start = jnp.where(outer == (par == 0), HALF, 0)

    def put(left_rows, left_obs):
        num, den = pair_sums(left_rows, left_obs, mate, mate_obs[...])
        send_a[0] = num
        send_a[1] = den

    @pl.when(kind_a & outer)
    def _():
        mate_obs[...] = observed(mate)
        left_rows = chunk(own, start)
        put(left_rows, observed(left_rows))

    @pl.when(kind_a & jnp.logical_not(outer))
    def _():
        at = pl.ds(pl.multiple_of(start, HALF), HALF)
        copies = [
            pltpu.make_async_copy(far.at[plane, at], far_v.at[plane], sems.at[plane]) for plane in range(3)
        ]
        for copy in copies:
            copy.start()
        mate_obs[...] = observed(mate)
        for copy in copies:
            copy.wait()
        put(far_v, observed(far_v))


def second_kernel(
    role, own, own_obs, mate, mate_obs, far, held_b, keep_a, keep_b, tri, send_d, keep_d, far_v, sems
):
    par, lo, core, beyond = role[0], role[1], role[2], role[3]
    outer = lo == par

    def rest(left, start):
        left_rows = chunk(left, start)
        num, den = pair_sums(left_rows, observed(left_rows), mate, mate_obs[...])
        held_b[0] = num
        held_b[1] = den

    @pl.when(core == par)
    def _():
        fetch(far, far_v, sems)
        for plane in range(3):
            arrived(far, far_v, sems, plane)
        put_tiles(tri, own, far_v, par, beyond)

        @pl.when(outer)
        def _():
            rest(own, jnp.where(par == 0, 0, HALF))
            put_rows(keep_a, keep_b, pair_sums(far_v, observed(far_v), mate, mate_obs[...]), par == 1)

        @pl.when(jnp.logical_not(outer))
        def _():
            rest(far_v, jnp.where(par == 1, 0, HALF))
            put_rows(keep_a, keep_b, pair_sums(own, own_obs[...], mate, mate_obs[...]), par == 0)

    @pl.when(core != par)
    def _():
        first = pair_sums(own, own_obs[...], own, own_obs[...])
        twin_obs = observed(mate)
        second = pair_sums(mate, twin_obs, mate, twin_obs)
        diag = (first[0] + second[0], first[1] + second[1])

        @pl.when(lo == 0)
        def _():
            for i in range(2):
                keep_d[i] = diag[i][:, :HALF]
                send_d[i] = diag[i][:, HALF:]

        @pl.when(lo == 1)
        def _():
            for i in range(2):
                send_d[i] = diag[i][:, :HALF]
                keep_d[i] = diag[i][:, HALF:]


def merge_kernel(role, held, kept, tri, tri_in, send, keep):
    par, lo, core = role[0], role[1], role[2]
    outer = lo == par
    row = lax.broadcasted_iota(jnp.int32, (HALF, HALF), 0)

    def near(source, target):
        first = jnp.where(par == 0, 0, HALF - role[5])
        free = (row >= first) & (row < first + role[5])
        for i in range(2):
            tile = (tri[i, :HALF] + tri_in[i, :HALF]).T
            other = (tri[i, HALF:] + tri_in[i, HALF:]).T

            @pl.when(par == 0)
            def _():
                target[i, :, HALF:] = jnp.where(free, tile, source[i, :, HALF:])
                target[i, :, :HALF] = jnp.where(free, other, source[i, :, :HALF])

            @pl.when(par == 1)
            def _():
                target[i, :, :HALF] = jnp.where(free, tile, source[i, :, :HALF])
                target[i, :, HALF:] = jnp.where(free, other, source[i, :, HALF:])

    def across(source, target):
        first = jnp.where(par == 0, HALF - role[6], 0)
        free = (row >= first) & (row < first + role[6])
        for i in range(2):
            tile = tri[i, :HALF] + tri_in[i, :HALF]
            other = tri[i, HALF:] + tri_in[i, HALF:]

            @pl.when(par == 0)
            def _():
                target[i, :, :HALF] = jnp.where(free, tile, source[i, :, :HALF])
                target[i, :, HALF:] = jnp.where(free, other, source[i, :, HALF:])

            @pl.when(par == 1)
            def _():
                target[i, :, HALF:] = jnp.where(free, tile, source[i, :, HALF:])
                target[i, :, :HALF] = jnp.where(free, other, source[i, :, :HALF])

    @pl.when((core == par) & outer)
    def _():
        near(held, send)
        across(kept, keep)

    @pl.when((core == par) & jnp.logical_not(outer))
    def _():
        across(held, send)
        near(kept, keep)


def ratio(num, den):
    return num / jnp.maximum(den, 1.0)


def ordered(first, second, i, swap):
    pair = (second[i], first[i]) if swap else (first[i], second[i])
    return jnp.concatenate(pair, axis=0)


def early_kernel(role, diag_in, diag, cut_a, cut_b, full_a, full_b, mirror_a, part, done, mine, other):
    par, lo, core, beyond = role[0], role[1], role[2], role[4]
    outer = lo == par

    def put_diag(target):
        target[:, :HALF] = ratio(diag[0] + diag_in[0], diag[1] + diag_in[1])

    def put_tiles_at(target, parity, source, flip):
        near_x = HALF if parity == 0 else 0
        near_z = HALF - near_x
        both = near_z if flip else near_x
        first, second = [
            ratio(source[0, :, at : at + HALF], source[1, :, at : at + HALF]).T
            for at in (both, HALF - both)
        ]

        def place(x, z, value):
            row, col = (z, x) if flip else (x, z)
            target[row : row + HALF, col : col + HALF] = value

        zero = jnp.zeros((HALF, HALF), F32)
        place(near_x, near_z, first)
        place(HALF - near_x, HALF - near_z, zero)

        @pl.when(beyond == 1)
        def _():
            place(near_x, HALF - near_z, second)
            place(HALF - near_x, near_z, zero)

        @pl.when(beyond == 0)
        def _():
            place(HALF - near_x, near_z, second)
            place(near_x, HALF - near_z, zero)

    def put_sums(sums, swap):
        at, rest = slice(0, HALF), slice(HALF, TILE)
        if swap:
            at, rest = rest, at
        done[...] = ratio(sums[0][:, at] + mirror_a[0].T, sums[1][:, at] + mirror_a[1].T)
        part[0] = sums[0][:, rest]
        part[1] = sums[1][:, rest]

    def when(parity, want_outer):
        return pl.when((par == parity) & (core == par) & (outer == want_outer))

    for parity in range(2):

        @when(parity, True)
        def _():
            put_sums([ordered(cut_a, cut_b, i, parity == 1) for i in range(2)], parity == 0)
            put_tiles_at(mine, parity, cut_b, True)
            put_diag(other)

        @when(parity, False)
        def _():
            put_sums([ordered(full_a, full_b, i, parity == 0) for i in range(2)], parity == 1)
            put_tiles_at(other, parity, full_b, False)
            put_diag(mine)


def ratio_kernel(role, part, done, mirror_b, send, keep):
    par, lo, core = role[0], role[1], role[2]
    outer = lo == par

    def when(parity, want_outer):
        return pl.when((par == parity) & (core == par) & (outer == want_outer))

    def value(parity, from_outer):
        swap = (parity == 0) == from_outer
        last = ratio(part[0] + mirror_b[0].T, part[1] + mirror_b[1].T)
        return jnp.concatenate([last, done[...]] if swap else [done[...], last], axis=1)

    @when(0, True)
    def _():
        result = value(0, True)
        keep[:, :128] = result[:, :128]
        send[...] = result[:, 128:]

    @when(1, True)
    def _():
        result = value(1, True)
        keep[:, :128] = result[:, 384:]
        send[...] = result[:, :384]

    @when(0, False)
    def _():
        result = value(0, False)
        keep[...] = result[:, :384]
        send[:, :128] = result[:, 384:]

    @when(1, False)
    def _():
        result = value(1, False)
        keep[...] = result[:, 128:]
        send[:, :128] = result[:, :128]


def place_kernel(role, row_cohort, col_cohort, keep, came, mine, other, out):
    par, lo, core = role[0], role[1], role[2]
    kind_a = core == par
    outer = lo == par
    rows = row_cohort[...]

    def when(parity, want_a, want_outer, parts):
        @pl.when((par == parity) & (kind_a == want_a) & (outer == want_outer))
        def _():
            start = 0
            for ref, width in parts:
                same = rows == col_cohort[:, start : start + width]
                out[:, start : start + width] = jnp.where(same, ref[:, :width], 0.0)
                start += width

    when(0, True, True, [(mine, 512), (keep, 128)])
    when(0, False, True, [(came, 384), (other, 256)])
    when(0, True, False, [(mine, 256), (keep, 384)])
    when(0, False, False, [(came, 128), (other, 512)])
    when(1, False, False, [(other, 512), (came, 128)])
    when(1, True, False, [(keep, 384), (mine, 256)])
    when(1, False, True, [(other, 256), (came, 384)])
    when(1, True, True, [(keep, 128), (mine, 512)])


def cohort_of(positions, cohort_ends):
    return jnp.sum((cohort_ends[None, :] <= positions[:, None]).astype(jnp.int32), axis=1)


def call(kernel, out_shapes, spaces, scratch=()):
    vmem = pl.BlockSpec(memory_space=pltpu.VMEM)
    return pl.pallas_call(
        kernel,
        out_shape=out_shapes,
        in_specs=[pl.BlockSpec(memory_space=pltpu.SMEM)] + [pl.BlockSpec(memory_space=space) for space in spaces],
        out_specs=jax.tree.map(lambda _: vmem, out_shapes),
        scratch_shapes=list(scratch),
        compiler_params=pltpu.CompilerParams(vmem_limit_bytes=VMEM),
    )


def per_device(probs, cohort_sizes):
    blocks = lax.axis_size("cohort")
    block = lax.axis_index("cohort")
    quarter = lax.axis_index("variant")
    par, lo, core = block % 2, quarter // 2, quarter % 2
    kind_a = core == par
    outer = lo == par
    cohort_ends = jnp.cumsum(cohort_sizes)

    def cohorts(start):
        position = start * TILE + jnp.arange(TILE, dtype=jnp.int32)
        return jnp.where(position < 0, -1, cohort_of(position, cohort_ends))

    step = jnp.where(par == 0, 2, -2)
    own_ids, ahead_ids, back_ids = cohorts(block), cohorts(block + step), cohorts(block - step)
    even = par == 0

    def split(ids, low):
        low_half, high_half = ids[:HALF], ids[HALF:]
        return jnp.where(low, low_half, high_half), jnp.where(low, high_half, low_half)

    def reach(x_ids, z_ids):
        x_near, _ = split(x_ids, jnp.logical_not(even))
        z_near, z_far = split(z_ids, even)
        x_edge = jnp.where(even, x_ids[-1], x_ids[0])
        z_edge = jnp.where(even, z_ids[0], z_ids[-1])
        beyond = jnp.any(z_far == x_edge)
        return jnp.sum(z_near == x_edge), jnp.sum(x_near == z_edge), beyond

    z_count, x_count, beyond_ahead = reach(own_ids, ahead_ids)
    _, _, beyond_back = reach(back_ids, own_ids)
    role = jnp.stack(
        [
            par,
            lo,
            core,
            jnp.where(kind_a, beyond_ahead, beyond_back),
            jnp.where(outer, beyond_back, beyond_ahead),
            z_count,
            x_count,
        ]
    ).astype(jnp.int32)

    def move(value, rule):
        return lax.ppermute(value, AXES, route(blocks, rule))

    far = move(probs, to_next)
    mate = move(probs, to_mate)
    half = jax.ShapeDtypeStruct((2, TILE, HALF), F32)
    rows = jax.ShapeDtypeStruct((2, HALF, TILE), F32)
    block_of = pltpu.VMEM(probs.shape, probs.dtype)
    planes = pltpu.SemaphoreType.DMA((3,))
    obs = jax.ShapeDtypeStruct(probs.shape[1:], probs.dtype)
    vmem = pltpu.VMEM
    own, own_obs = call(stage_kernel, (jax.ShapeDtypeStruct(probs.shape, probs.dtype), obs), [vmem])(
        role, probs
    )
    send_t = call(tiles_kernel, half, (vmem, pl.ANY), (block_of, planes))(role, own, far)
    chunk_of = pltpu.VMEM((3, HALF, probs.shape[2]), probs.dtype)
    send_a, mate_obs = call(
        first_kernel, (rows, obs), (vmem, vmem, vmem, pl.ANY, pl.ANY), (chunk_of, planes)
    )(role, own, own_obs, mate, far, send_t)
    tri_in = move(send_t, to_far)
    came_a = move(send_a, to_chip)
    held_b, keep_a, kept_b, tri, send_d, keep_d = call(
        second_kernel,
        (rows, rows, rows, half, half, half),
        (vmem, vmem, vmem, vmem, pl.ANY),
        (block_of, planes),
    )(role, own, own_obs, mate, mate_obs, far)
    send_b, keep_b = call(merge_kernel, (rows, rows), [pltpu.VMEM] * 4)(role, held_b, kept_b, tri, tri_in)
    came_b = move(send_b, to_chip)
    full_a = keep_a + came_a
    mirror_a = move(full_a, to_mirror)
    cut_a = move(full_a, to_cut)
    send_d, keep_d, came_b = lax.optimization_barrier((send_d, keep_d, came_b))
    diag_in = move(send_d, to_across)
    full_b = keep_b + came_b
    cut_b = move(full_b, to_cut)
    mirror_b = move(full_b, to_mirror)
    diag = move(keep_d, to_side)
    wide = jax.ShapeDtypeStruct((TILE, WIDTH), F32)
    square = jax.ShapeDtypeStruct((TILE, TILE), F32)
    column = jax.ShapeDtypeStruct((TILE, HALF), F32)
    narrow = jax.ShapeDtypeStruct((TILE, 384), F32)
    part, done, mine, other = call(early_kernel, (half, column, square, square), [vmem] * 7)(
        role, diag_in, diag, cut_a, cut_b, full_a, full_b, mirror_a
    )
    other = move(other, to_core)
    send, keep = call(ratio_kernel, (narrow, narrow), [vmem] * 3)(role, part, done, mirror_b)
    came = move(send, to_core)

    col_pos = (block - 2) * TILE + quarter * WIDTH + jnp.arange(WIDTH, dtype=jnp.int32)
    inside = (col_pos >= 0) & (col_pos < TILE * blocks)
    row_cohort = own_ids[:, None]
    col_cohort = jnp.where(inside, cohort_of(col_pos, cohort_ends), -1)[None, :]
    return call(place_kernel, wide, [vmem] * 6)(
        role, row_cohort, col_cohort, keep, came, mine, other
    )


def solution(mesh):
    return jax.shard_map(
        per_device,
        mesh=mesh,
        in_specs=(P(None, "cohort", "variant"), P()),
        out_specs=P("cohort", "variant"),
        check_vma=False,
    )
```

```python
import jax
import jax.numpy as jnp
from jax import lax
from jax.experimental import pallas as pl
from jax.experimental.pallas import tpu as pltpu
from jax.sharding import PartitionSpec as P

AXES = ("cohort", "variant")
TILE = 512
HALF = 256
WIDTH = 640
F32 = jnp.float32
VMEM = 24 * 1024 * 1024


def route(blocks, rule):
    pairs = []
    for k in range(blocks // 2):
        for par in range(2):
            for lo in range(2):
                for core in range(2):
                    to = rule(k, par, lo, core)
                    if to is not None and 0 <= to[0] < blocks // 2:
                        source = (2 * k + par) * 4 + lo * 2 + core
                        pairs.append((source, (2 * to[0] + to[1]) * 4 + to[2] * 2 + to[3]))
    return pairs


def is_a(par, core):
    return core == par


def is_outer(par, lo):
    return lo == par


def to_mate(k, par, lo, core):
    if is_a(par, core):
        return (k, par, lo, 1 - core)
    return (k, 1 - par, lo, core)


def to_next(k, par, lo, core):
    return (k - 1 if core == 0 else k + 1, par, lo, core)


def to_chip(k, par, lo, core):
    return (k, par, 1 - lo, core) if is_a(par, core) else None


def to_across(k, par, lo, core):
    return None if is_a(par, core) else (k, par, 1 - lo, 1 - core)


def to_side(k, par, lo, core):
    return None if is_a(par, core) else (k, par, lo, 1 - core)


def to_far(k, par, lo, core):
    if is_a(par, core):
        return None
    return (k + 1 if core == 0 else k - 1, par, lo, 1 - core)


def to_mirror(k, par, lo, core):
    return (k, 1 - par, 1 - lo, 1 - core) if is_a(par, core) else None


def to_cut(k, par, lo, core):
    if is_a(par, core) and is_outer(par, lo):
        return (k + 1 if par == 0 else k - 1, par, lo, core)
    return None


def to_core(k, par, lo, core):
    return (k, par, lo, 1 - core) if is_a(par, core) else None


def dot_t(left, right):
    return lax.dot_general(left, right, (((1,), (1,)), ((), ())), preferred_element_type=F32)


def observed(data):
    total = data[0].astype(F32) + data[1].astype(F32) + data[2].astype(F32)
    return total.astype(jnp.bfloat16)


def pair_sums(left, left_obs, right, right_obs):
    cross = dot_t(left[0], right[2]) + dot_t(left[2], right[0])
    num = dot_t(left[1], right[1]) - 2.0 * cross
    den = dot_t(left[1], right_obs) + dot_t(left_obs, right[1])
    return num, den


def put_rows(first, second, values, swap):
    @pl.when(swap)
    def _():
        for i in range(2):
            first[i] = values[i][HALF:]
            second[i] = values[i][:HALF]

    @pl.when(jnp.logical_not(swap))
    def _():
        for i in range(2):
            first[i] = values[i][:HALF]
            second[i] = values[i][HALF:]


def put_tiles(tri, left, right, par, beyond):
    near_left = jnp.where(par == 0, HALF, 0)
    near_right = HALF - near_left
    other_left = jnp.where(beyond == 1, near_left, near_right)
    other_right = jnp.where(beyond == 1, near_left, near_right)

    def rows(data, start):
        at = pl.ds(pl.multiple_of(start, HALF), HALF)
        return [data[plane, at, :] for plane in range(3)]

    for tile, (l, r) in enumerate(((near_left, near_right), (other_left, other_right))):
        left_rows, right_rows = rows(left, l), rows(right, r)
        num, den = pair_sums(left_rows, observed(left_rows), right_rows, observed(right_rows))
        tri[0, tile * HALF : (tile + 1) * HALF] = num
        tri[1, tile * HALF : (tile + 1) * HALF] = den


def fetch(source, target, sems, order=(1, 0, 2)):
    for plane in order:
        pltpu.make_async_copy(source.at[plane], target.at[plane], sems.at[plane]).start()


def arrived(source, target, sems, plane):
    pltpu.make_async_copy(source.at[plane], target.at[plane], sems.at[plane]).wait()


def stage_kernel(role, own, out, out_obs):
    out[...] = own[...]
    out_obs[...] = observed(own)


def tiles_kernel(role, own, far, tri, far_v, sems):
    par, core, beyond = role[0], role[2], role[3]

    @pl.when(core != par)
    def _():
        fetch(far, far_v, sems)
        for plane in range(3):
            arrived(far, far_v, sems, plane)
        put_tiles(tri, far_v, own, par, beyond)


def chunk(data, start):
    at = pl.ds(pl.multiple_of(start, HALF), HALF)
    return [data[plane, at, :] for plane in range(3)]


def first_kernel(role, own, own_obs, mate, far, after, send_a, mate_obs, far_v, sems):
    par, lo, core = role[0], role[1], role[2]
    kind_a = core == par
    outer = lo == par
    start = jnp.where(outer == (par == 0), HALF, 0)

    def put(left_rows, left_obs):
        num, den = pair_sums(left_rows, left_obs, mate, mate_obs[...])
        send_a[0] = num
        send_a[1] = den

    @pl.when(kind_a & outer)
    def _():
        mate_obs[...] = observed(mate)
        left_rows = chunk(own, start)
        put(left_rows, observed(left_rows))

    @pl.when(kind_a & jnp.logical_not(outer))
    def _():
        at = pl.ds(pl.multiple_of(start, HALF), HALF)
        copies = [
            pltpu.make_async_copy(far.at[plane, at], far_v.at[plane], sems.at[plane]) for plane in range(3)
        ]
        for copy in copies:
            copy.start()
        mate_obs[...] = observed(mate)
        for copy in copies:
            copy.wait()
        put(far_v, observed(far_v))


def second_kernel(
    role, own, own_obs, mate, mate_obs, far, held_b, keep_a, keep_b, tri, send_d, keep_d, far_v, sems
):
    par, lo, core, beyond = role[0], role[1], role[2], role[3]
    outer = lo == par

    def rest(left, start):
        left_rows = chunk(left, start)
        num, den = pair_sums(left_rows, observed(left_rows), mate, mate_obs[...])
        held_b[0] = num
        held_b[1] = den

    @pl.when(core == par)
    def _():
        fetch(far, far_v, sems)
        for plane in range(3):
            arrived(far, far_v, sems, plane)
        put_tiles(tri, own, far_v, par, beyond)

        @pl.when(outer)
        def _():
            rest(own, jnp.where(par == 0, 0, HALF))
            put_rows(keep_a, keep_b, pair_sums(far_v, observed(far_v), mate, mate_obs[...]), par == 1)

        @pl.when(jnp.logical_not(outer))
        def _():
            rest(far_v, jnp.where(par == 1, 0, HALF))
            put_rows(keep_a, keep_b, pair_sums(own, own_obs[...], mate, mate_obs[...]), par == 0)

    @pl.when(core != par)
    def _():
        first = pair_sums(own, own_obs[...], own, own_obs[...])
        twin_obs = observed(mate)
        second = pair_sums(mate, twin_obs, mate, twin_obs)
        diag = (first[0] + second[0], first[1] + second[1])

        @pl.when(lo == 0)
        def _():
            for i in range(2):
                keep_d[i] = diag[i][:, :HALF]
                send_d[i] = diag[i][:, HALF:]

        @pl.when(lo == 1)
        def _():
            for i in range(2):
                send_d[i] = diag[i][:, :HALF]
                keep_d[i] = diag[i][:, HALF:]


def merge_kernel(role, held, kept, tri, tri_in, send, keep):
    par, lo, core = role[0], role[1], role[2]
    outer = lo == par
    row = lax.broadcasted_iota(jnp.int32, (HALF, HALF), 0)

    def near(source, target):
        first = jnp.where(par == 0, 0, HALF - role[5])
        free = (row >= first) & (row < first + role[5])
        for i in range(2):
            tile = (tri[i, :HALF] + tri_in[i, :HALF]).T
            other = (tri[i, HALF:] + tri_in[i, HALF:]).T

            @pl.when(par == 0)
            def _():
                target[i, :, HALF:] = jnp.where(free, tile, source[i, :, HALF:])
                target[i, :, :HALF] = jnp.where(free, other, source[i, :, :HALF])

            @pl.when(par == 1)
            def _():
                target[i, :, :HALF] = jnp.where(free, tile, source[i, :, :HALF])
                target[i, :, HALF:] = jnp.where(free, other, source[i, :, HALF:])

    def across(source, target):
        first = jnp.where(par == 0, HALF - role[6], 0)
        free = (row >= first) & (row < first + role[6])
        for i in range(2):
            tile = tri[i, :HALF] + tri_in[i, :HALF]
            other = tri[i, HALF:] + tri_in[i, HALF:]

            @pl.when(par == 0)
            def _():
                target[i, :, :HALF] = jnp.where(free, tile, source[i, :, :HALF])
                target[i, :, HALF:] = jnp.where(free, other, source[i, :, HALF:])

            @pl.when(par == 1)
            def _():
                target[i, :, HALF:] = jnp.where(free, tile, source[i, :, HALF:])
                target[i, :, :HALF] = jnp.where(free, other, source[i, :, :HALF])

    @pl.when((core == par) & outer)
    def _():
        near(held, send)
        across(kept, keep)

    @pl.when((core == par) & jnp.logical_not(outer))
    def _():
        across(held, send)
        near(kept, keep)


def ratio(num, den):
    return num / jnp.maximum(den, 1.0)


def ordered(first, second, i, swap):
    pair = (second[i], first[i]) if swap else (first[i], second[i])
    return jnp.concatenate(pair, axis=0)


def early_kernel(role, diag_in, diag, cut_a, cut_b, full_a, full_b, mirror_a, part, done, mine, other):
    par, lo, core, beyond = role[0], role[1], role[2], role[4]
    outer = lo == par

    def put_diag(target):
        target[:, :HALF] = ratio(diag[0] + diag_in[0], diag[1] + diag_in[1])

    def put_tiles_at(target, parity, source, flip):
        near_x = HALF if parity == 0 else 0
        near_z = HALF - near_x
        both = near_z if flip else near_x
        first, second = [
            ratio(source[0, :, at : at + HALF], source[1, :, at : at + HALF]).T
            for at in (both, HALF - both)
        ]

        def place(x, z, value):
            row, col = (z, x) if flip else (x, z)
            target[row : row + HALF, col : col + HALF] = value

        zero = jnp.zeros((HALF, HALF), F32)
        place(near_x, near_z, first)
        place(HALF - near_x, HALF - near_z, zero)

        @pl.when(beyond == 1)
        def _():
            place(near_x, HALF - near_z, second)
            place(HALF - near_x, near_z, zero)

        @pl.when(beyond == 0)
        def _():
            place(HALF - near_x, near_z, second)
            place(near_x, HALF - near_z, zero)

    def put_sums(sums, swap):
        at, rest = slice(0, HALF), slice(HALF, TILE)
        if swap:
            at, rest = rest, at
        done[...] = ratio(sums[0][:, at] + mirror_a[0].T, sums[1][:, at] + mirror_a[1].T)
        part[0] = sums[0][:, rest]
        part[1] = sums[1][:, rest]

    def when(parity, want_outer):
        return pl.when((par == parity) & (core == par) & (outer == want_outer))

    for parity in range(2):

        @when(parity, True)
        def _():
            put_sums([ordered(cut_a, cut_b, i, parity == 1) for i in range(2)], parity == 0)
            put_tiles_at(mine, parity, cut_b, True)
            put_diag(other)

        @when(parity, False)
        def _():
            put_sums([ordered(full_a, full_b, i, parity == 0) for i in range(2)], parity == 1)
            put_tiles_at(other, parity, full_b, False)
            put_diag(mine)


def ratio_kernel(role, part, done, mirror_b, send, keep):
    par, lo, core = role[0], role[1], role[2]
    outer = lo == par

    def when(parity, want_outer):
        return pl.when((par == parity) & (core == par) & (outer == want_outer))

    def value(parity, from_outer):
        swap = (parity == 0) == from_outer
        last = ratio(part[0] + mirror_b[0].T, part[1] + mirror_b[1].T)
        return jnp.concatenate([last, done[...]] if swap else [done[...], last], axis=1)

    @when(0, True)
    def _():
        result = value(0, True)
        keep[:, :128] = result[:, :128]
        send[...] = result[:, 128:]

    @when(1, True)
    def _():
        result = value(1, True)
        keep[:, :128] = result[:, 384:]
        send[...] = result[:, :384]

    @when(0, False)
    def _():
        result = value(0, False)
        keep[...] = result[:, :384]
        send[:, :128] = result[:, 384:]

    @when(1, False)
    def _():
        result = value(1, False)
        keep[...] = result[:, 128:]
        send[:, :128] = result[:, :128]


def place_kernel(role, row_cohort, col_cohort, keep, came, mine, other, out):
    par, lo, core = role[0], role[1], role[2]
    kind_a = core == par
    outer = lo == par
    rows = row_cohort[...]

    def when(parity, want_a, want_outer, parts):
        @pl.when((par == parity) & (kind_a == want_a) & (outer == want_outer))
        def _():
            start = 0
            for ref, width in parts:
                same = rows == col_cohort[:, start : start + width]
                out[:, start : start + width] = jnp.where(same, ref[:, :width], 0.0)
                start += width

    when(0, True, True, [(mine, 512), (keep, 128)])
    when(0, False, True, [(came, 384), (other, 256)])
    when(0, True, False, [(mine, 256), (keep, 384)])
    when(0, False, False, [(came, 128), (other, 512)])
    when(1, False, False, [(other, 512), (came, 128)])
    when(1, True, False, [(keep, 384), (mine, 256)])
    when(1, False, True, [(other, 256), (came, 384)])
    when(1, True, True, [(keep, 128), (mine, 512)])


def cohort_of(positions, cohort_ends):
    return jnp.sum((cohort_ends[None, :] <= positions[:, None]).astype(jnp.int32), axis=1)


def call(kernel, out_shapes, spaces, scratch=()):
    vmem = pl.BlockSpec(memory_space=pltpu.VMEM)
    return pl.pallas_call(
        kernel,
        out_shape=out_shapes,
        in_specs=[pl.BlockSpec(memory_space=pltpu.SMEM)] + [pl.BlockSpec(memory_space=space) for space in spaces],
        out_specs=jax.tree.map(lambda _: vmem, out_shapes),
        scratch_shapes=list(scratch),
        compiler_params=pltpu.CompilerParams(vmem_limit_bytes=VMEM),
    )


def per_device(probs, cohort_sizes):
    blocks = lax.axis_size("cohort")
    block = lax.axis_index("cohort")
    quarter = lax.axis_index("variant")
    par, lo, core = block % 2, quarter // 2, quarter % 2
    kind_a = core == par
    outer = lo == par
    cohort_ends = jnp.cumsum(cohort_sizes)

    def cohorts(start):
        position = start * TILE + jnp.arange(TILE, dtype=jnp.int32)
        return jnp.where(position < 0, -1, cohort_of(position, cohort_ends))

    step = jnp.where(par == 0, 2, -2)
    own_ids, ahead_ids, back_ids = cohorts(block), cohorts(block + step), cohorts(block - step)
    even = par == 0

    def split(ids, low):
        low_half, high_half = ids[:HALF], ids[HALF:]
        return jnp.where(low, low_half, high_half), jnp.where(low, high_half, low_half)

    def reach(x_ids, z_ids):
        x_near, _ = split(x_ids, jnp.logical_not(even))
        z_near, z_far = split(z_ids, even)
        x_edge = jnp.where(even, x_ids[-1], x_ids[0])
        z_edge = jnp.where(even, z_ids[0], z_ids[-1])
        beyond = jnp.any(z_far == x_edge)
        return jnp.sum(z_near == x_edge), jnp.sum(x_near == z_edge), beyond

    z_count, x_count, beyond_ahead = reach(own_ids, ahead_ids)
    _, _, beyond_back = reach(back_ids, own_ids)
    role = jnp.stack(
        [
            par,
            lo,
            core,
            jnp.where(kind_a, beyond_ahead, beyond_back),
            jnp.where(outer, beyond_back, beyond_ahead),
            z_count,
            x_count,
        ]
    ).astype(jnp.int32)

    def move(value, rule):
        return lax.ppermute(value, AXES, route(blocks, rule))

    far = move(probs, to_next)
    mate = move(probs, to_mate)
    half = jax.ShapeDtypeStruct((2, TILE, HALF), F32)
    rows = jax.ShapeDtypeStruct((2, HALF, TILE), F32)
    block_of = pltpu.VMEM(probs.shape, probs.dtype)
    planes = pltpu.SemaphoreType.DMA((3,))
    obs = jax.ShapeDtypeStruct(probs.shape[1:], probs.dtype)
    vmem = pltpu.VMEM
    own, own_obs = call(stage_kernel, (jax.ShapeDtypeStruct(probs.shape, probs.dtype), obs), [vmem])(
        role, probs
    )
    send_t = call(tiles_kernel, half, (vmem, pl.ANY), (block_of, planes))(role, own, far)
    chunk_of = pltpu.VMEM((3, HALF, probs.shape[2]), probs.dtype)
    send_a, mate_obs = call(
        first_kernel, (rows, obs), (vmem, vmem, vmem, pl.ANY, pl.ANY), (chunk_of, planes)
    )(role, own, own_obs, mate, far, send_t)
    tri_in = move(send_t, to_far)
    came_a = move(send_a, to_chip)
    held_b, keep_a, kept_b, tri, send_d, keep_d = call(
        second_kernel,
        (rows, rows, rows, half, half, half),
        (vmem, vmem, vmem, vmem, pl.ANY),
        (block_of, planes),
    )(role, own, own_obs, mate, mate_obs, far)
    send_b, keep_b = call(merge_kernel, (rows, rows), [pltpu.VMEM] * 4)(role, held_b, kept_b, tri, tri_in)
    came_b = move(send_b, to_chip)
    full_a = keep_a + came_a
    mirror_a = move(full_a, to_mirror)
    cut_a = move(full_a, to_cut)
    send_d, came_b = lax.optimization_barrier((send_d, came_b))
    diag_in = move(send_d, to_across)
    full_b = keep_b + came_b
    cut_b = move(full_b, to_cut)
    mirror_b = move(full_b, to_mirror)
    diag = move(keep_d, to_side)
    wide = jax.ShapeDtypeStruct((TILE, WIDTH), F32)
    square = jax.ShapeDtypeStruct((TILE, TILE), F32)
    column = jax.ShapeDtypeStruct((TILE, HALF), F32)
    narrow = jax.ShapeDtypeStruct((TILE, 384), F32)
    part, done, mine, other = call(early_kernel, (half, column, square, square), [vmem] * 7)(
        role, diag_in, diag, cut_a, cut_b, full_a, full_b, mirror_a
    )
    other = move(other, to_core)
    send, keep = call(ratio_kernel, (narrow, narrow), [vmem] * 3)(role, part, done, mirror_b)
    came = move(send, to_core)

    col_pos = (block - 2) * TILE + quarter * WIDTH + jnp.arange(WIDTH, dtype=jnp.int32)
    inside = (col_pos >= 0) & (col_pos < TILE * blocks)
    row_cohort = own_ids[:, None]
    col_cohort = jnp.where(inside, cohort_of(col_pos, cohort_ends), -1)[None, :]
    return call(place_kernel, wide, [vmem] * 6)(
        role, row_cohort, col_cohort, keep, came, mine, other
    )


def solution(mesh):
    return jax.shard_map(
        per_device,
        mesh=mesh,
        in_specs=(P(None, "cohort", "variant"), P()),
        out_specs=P("cohort", "variant"),
        check_vma=False,
    )
```
